32 devices in a mesh: sec: 4 (over x, core), col: 8 (over z, y).
Axes of the slice: x: 2, y: 2, z: 4, core: 2. Of those that a mesh axis runs over, the one named last changes fastest.
Arguments:
- rhs: bfloat16 [256, 64, 256], P(('sec', 'col')), may hold values from -6 to 6
- diag_inv: bfloat16 [256, 64, 64], P(('sec', 'col')), may hold values from -0.5 to 0.5
- off_tiles: bfloat16 [256, 16, 64, 64], P(('sec', 'col')), may hold values from -0.1875 to 0.1875
- targets: int32 [256, 16], P(('sec', 'col')), may hold values from 0 to 63, all different within a row
- row_slot: int32 [4, 64], P('sec'), may hold values from 0 to 63, each once within a row
Outputs:
- solution: bfloat16 [256, 64, 256], P(('sec', 'col'))
- handed_on: bfloat16 [256, 64, 256], P(('sec', 'col'))
The draws below stay inside these ranges and needn't reach their ends.
Inputs may be any that keep to these rules, and one draw needn't show every extreme that they name: The 16 targets of one block are distinct. `row_slot`: each row is a permutation.
All inputs are finite; a program needn't handle non-finite values.
Results may differ from the reference program's by a relative error of at most 0.03.
Values may be sent and summed in bfloat16 or wider, within the bound.
A program may use at most 64 MiB of HBM per device.

```python
import jax
import jax.numpy as jnp
from jax import lax

W = 64
NRHS = 256
NOFF = 16
BPD = 8
NB_SEC = 64
NBLK = 256
N_SEC = 4
N_COL = 8


def level_of(rng, dims, pieces, low, largest):
    gain, own = 1.0, jax.random.fold_in(rng, 6)
    for dim, shards_of in pieces:
        steps = jnp.exp(jax.random.uniform(jax.random.fold_in(own, dim), (shards_of,), jnp.float32, low / len(pieces), largest / len(pieces)))
        gain = gain * jnp.repeat(steps, dims[dim] // shards_of).reshape([-1 if axis == dim else 1 for axis in range(len(dims))])
    return gain


def distinct(rng, rows, amount, top, lift):
    order = jax.random.permutation(jax.random.fold_in(rng, 1), amount)
    favour = order
    for power in range(3):
        favour = favour * favour // amount
    favour = favour * lift // amount
    lots = jax.random.randint(jax.random.fold_in(rng, 2), (rows, amount), 0, 4096) + favour
    holders = jax.random.permutation(jax.random.fold_in(rng, 3), rows)[jnp.arange(amount) % rows]
    lots = jnp.where(jnp.arange(rows)[:, None] == holders[None, :], 1 << 14, lots)
    score = lots * amount + jnp.arange(amount)
    return lax.top_k(score.astype(jnp.int32), top)[1].astype(jnp.int32)


def scatter_about(stream_key, dims, scale, bound, cuts=(), dtype=jnp.bfloat16):
    result = jax.random.normal(stream_key, dims, jnp.float32) * scale
    if len(cuts) > 0:
        result = level_of(stream_key, dims, cuts, -0.22, 0.18) * result
    return jnp.clip(result, min=-bound, max=bound).astype(dtype)


def setup_inputs(seed: int = 0) -> dict:
    seeds = jax.random.split(jax.random.key(seed), 6)
    rhs = scatter_about(seeds[0], (NBLK, W, NRHS), 1.0, 6.0, ((0, 32),))
    diag_inv = scatter_about(seeds[1], (NBLK, W, W), (2 * W) ** -0.5, 0.5, ((0, 32),))
    off_tiles = scatter_about(seeds[2], (NBLK, NOFF, W, W), (W * NOFF) ** -0.5, 0.1875, ((0, 32),))
    targets = distinct(seeds[3], NBLK, NB_SEC, NOFF, 4096)
    row_slot = jax.vmap(lambda own: jax.random.permutation(own, NB_SEC))(jax.random.split(seeds[4], N_SEC)).reshape((N_SEC, NB_SEC)).astype(jnp.int32)
    return dict(rhs=rhs, diag_inv=diag_inv, off_tiles=off_tiles, targets=targets, row_slot=row_slot)


def reference(rhs, diag_inv, off_tiles, targets, row_slot):
    count = NB_SEC
    incoming = jnp.zeros((count, W, NRHS), jnp.bfloat16)
    solved_all = []
    handed_all = []
    for section in range(N_SEC):
        start = section * count
        residual = (rhs[start:start + count].astype(jnp.float32) - incoming.astype(jnp.float32)).astype(jnp.bfloat16)
        solved = jnp.einsum("kab,kbn->kan", diag_inv[start:start + count].astype(jnp.float32), residual.astype(jnp.float32)).astype(jnp.bfloat16)
        tiles = jnp.einsum("kpab,kbn->kpan", off_tiles[start:start + count].astype(jnp.float32), solved.astype(jnp.float32)).astype(jnp.bfloat16)
        dest_slot = row_slot[section][targets[start:start + count]]
        tiles = tiles.reshape(N_COL, BPD * NOFF, W, NRHS)
        dest_slot = dest_slot.reshape(N_COL, BPD * NOFF).astype(jnp.int32)

        def device_sum(carry, item):
            piece, slots = item
            partial_value = jnp.zeros((count, W, NRHS), jnp.float32).at[slots].add(piece.astype(jnp.float32))
            rounded = lax.optimization_barrier(partial_value.astype(jnp.bfloat16))
            return carry + rounded.astype(jnp.float32), None

        total, _ = lax.scan(device_sum, jnp.zeros((count, W, NRHS), jnp.float32), (tiles, dest_slot))
        incoming = total.astype(jnp.bfloat16)
        solved_all.append(solved)
        handed_all.append(incoming)
    return jnp.concatenate(solved_all, 0), jnp.concatenate(handed_all, 0)
```

```python
import functools

import jax
import jax.numpy as jnp
from jax import lax
from jax.experimental import pallas as pl
from jax.experimental.pallas import tpu as pltpu
from jax.sharding import PartitionSpec as P

MESH = pl.DeviceIdType.MESH


def low_size(n_col):
    low = 1
    while (2 * low) ** 2 <= n_col:
        low *= 2
    return low


def kernel(
    dims, idx_ref, rhs_ref, diag_ref, off_ref, sol_ref, hand_ref,
    a_ref, x_ref, inc, send1, recv1, send2, recv2, acc, passed,
    s1_sem, r1_sem, s2_sem, r2_sem, sp_sem, rp_sem,
):
    n_sec, n_hi, n_lo, chunks, nc = dims
    blocks, width, _ = rhs_ref.shape
    noff = off_ref.shape[1]
    rows = idx_ref.shape[1]
    sec = lax.axis_index("sec")
    col = lax.axis_index("col")
    hi, lo = col // n_lo, col % n_lo
    size = blocks * width

    def lo_peer(o):
        return {"sec": sec, "col": hi * n_lo + lax.rem(lo + o, n_lo)}

    def hi_peer(o):
        return {"sec": sec, "col": lax.rem(hi + o, n_hi) * n_lo + lo}

    def next_sec():
        return {"sec": lax.rem(sec + 1, n_sec), "col": col}

    barrier = pltpu.get_barrier_semaphore()
    for o in range(1, n_lo):
        pl.semaphore_signal(barrier, inc=1, device_id=lo_peer(o), device_id_type=MESH)
    for o in range(1, n_hi):
        pl.semaphore_signal(barrier, inc=1, device_id=hi_peer(o), device_id_type=MESH)

    for by in (1, n_sec - 1):
        pl.semaphore_signal(
            barrier, inc=1, device_id={"sec": lax.rem(sec + by, n_sec), "col": col},
            device_id_type=MESH,
        )

    @pl.when(sec == 0)
    def _():
        inc[...] = jnp.zeros_like(inc)

    def build(i, carry):
        for pair in range(blocks // 2):
            parts = []
            for k in (2 * pair, 2 * pair + 1):
                p = idx_ref[k, i]
                tile = off_ref[k, jnp.minimum(p, noff - 1)]
                parts.append(jnp.where(p < noff, tile, jnp.zeros_like(tile)))
            a_ref[i, :, 2 * pair * width:2 * (pair + 1) * width] = jnp.concatenate(parts, axis=1)
        return carry

    lax.fori_loop(0, rows, build, 0)

    pl.semaphore_wait(barrier, n_lo - 1 + n_hi - 1 + 2)

    def copy1(j, o, oh):
        return pltpu.make_async_remote_copy(
            src_ref=send1.at[j, o - 1, oh], dst_ref=recv1.at[j, o - 1, oh],
            send_sem=s1_sem.at[j, o - 1, oh], recv_sem=r1_sem.at[j, o - 1, oh],
            device_id=lo_peer(o), device_id_type=MESH,
        )

    def copy2(j, oh):
        return pltpu.make_async_remote_copy(
            src_ref=send2.at[j, oh - 1], dst_ref=recv2.at[j, oh - 1],
            send_sem=s2_sem.at[j, oh - 1], recv_sem=r2_sem.at[j, oh - 1],
            device_id=hi_peer(oh), device_id_type=MESH,
        )

    def copyp(j):
        return pltpu.make_async_remote_copy(
            src_ref=passed.at[j], dst_ref=inc.at[j],
            send_sem=sp_sem.at[j], recv_sem=rp_sem.at[j],
            device_id=next_sec(), device_id_type=MESH,
        )

    order = list(range(1, n_hi)) + [0]

    def product(j, oh, o):
        dest = lax.rem(hi + oh, n_hi) * n_lo + lax.rem(lo + o, n_lo)
        a = a_ref[pl.ds(dest * blocks, blocks)].reshape(size, size)
        return jnp.dot(a, x_ref[j], preferred_element_type=jnp.float32)

    def first(j):
        @pl.when(sec > 0)
        def _():
            copyp(j).wait_recv()

        cols = slice(j * nc, (j + 1) * nc)
        for k in range(blocks):
            part = slice(k * width, (k + 1) * width)
            residual = (
                rhs_ref[k, :, cols].astype(jnp.float32) - inc[j, part, :].astype(jnp.float32)
            ).astype(jnp.bfloat16)
            solved = jnp.dot(
                diag_ref[k], residual, preferred_element_type=jnp.float32
            ).astype(jnp.bfloat16)
            x_ref[j, part, :] = solved
            sol_ref[k, :, cols] = solved
        for oh in order:
            for o in range(1, n_lo):
                send1[j, o - 1, oh] = product(j, oh, o).astype(jnp.bfloat16)
                copy1(j, o, oh).start()

    def middle(j):
        for oh in order:
            total = product(j, oh, 0)
            for o in range(1, n_lo):
                copy1(j, o, oh).wait_recv()
                total = total + recv1[j, o - 1, oh].astype(jnp.float32)
            if oh == 0:
                acc[j] = total
            else:
                send2[j, oh - 1] = total.astype(jnp.bfloat16)
                copy2(j, oh).start()

    def last(j):
        total = acc[j]
        for oh in range(1, n_hi):
            copy2(j, oh).wait_recv()
            total = total + recv2[j, oh - 1].astype(jnp.float32)
        passed[j] = total.astype(jnp.bfloat16)

        @pl.when(sec < n_sec - 1)
        def _():
            copyp(j).start()

        hand_ref[:, :, j * nc:(j + 1) * nc] = passed[j].reshape(blocks, width, nc)

    first(0)
    middle(0)
    for j in range(chunks):
        if j + 1 < chunks:
            first(j + 1)
        last(j)
        if j + 1 < chunks:
            middle(j + 1)

    for j in range(chunks):
        for o in range(1, n_lo):
            for oh in range(n_hi):
                copy1(j, o, oh).wait_send()
        for oh in range(1, n_hi):
            copy2(j, oh).wait_send()

        @pl.when(sec < n_sec - 1)
        def _():
            copyp(j).wait_send()


def shards(n_sec, n_col, rhs, diag_inv, off_tiles, targets, row_slot):
    blocks, width, columns = rhs.shape
    noff = off_tiles.shape[1]
    rows = row_slot.shape[1]
    n_lo = low_size(n_col)
    n_hi = n_col // n_lo
    nc = 128
    chunks = columns // nc
    size = blocks * width
    hit = (targets[:, None, :, None] == jnp.arange(rows, dtype=jnp.int32)[None, None, None, :]) & (
        row_slot[0][None, None, None, :] == jnp.arange(rows, dtype=jnp.int32)[None, :, None, None]
    )
    place = jnp.arange(noff, dtype=jnp.int32)[None, None, :, None]
    idx = jnp.min(jnp.where(hit, place, noff), axis=(2, 3))

    vmem = pl.BlockSpec(memory_space=pltpu.VMEM)
    out = jax.ShapeDtypeStruct((blocks, width, columns), jnp.bfloat16)
    dma = pltpu.SemaphoreType.DMA
    bf16 = jnp.bfloat16
    return pl.pallas_call(
        functools.partial(kernel, (n_sec, n_hi, n_lo, chunks, nc)),
        out_shape=(out, out),
        in_specs=[pl.BlockSpec(memory_space=pltpu.SMEM), vmem, vmem, vmem],
        out_specs=(vmem, vmem),
        scratch_shapes=[
            pltpu.VMEM((rows, width, size), bf16),
            pltpu.VMEM((chunks, size, nc), bf16),
            pltpu.VMEM((chunks, size, nc), bf16),
            pltpu.VMEM((chunks, n_lo - 1, n_hi, size, nc), bf16),
            pltpu.VMEM((chunks, n_lo - 1, n_hi, size, nc), bf16),
            pltpu.VMEM((chunks, n_hi - 1, size, nc), bf16),
            pltpu.VMEM((chunks, n_hi - 1, size, nc), bf16),
            pltpu.VMEM((chunks, size, nc), jnp.float32),
            pltpu.VMEM((chunks, size, nc), bf16),
            dma((chunks, n_lo - 1, n_hi)),
            dma((chunks, n_lo - 1, n_hi)),
            dma((chunks, n_hi - 1)),
            dma((chunks, n_hi - 1)),
            dma((chunks,)),
            dma((chunks,)),
        ],
        compiler_params=pltpu.CompilerParams(
            collective_id=0, has_side_effects=True, vmem_limit_bytes=40 * 1024 * 1024
        ),
    )(idx, rhs, diag_inv, off_tiles)


def solution(mesh):
    return jax.shard_map(
        functools.partial(shards, mesh.shape["sec"], mesh.shape["col"]),
        mesh=mesh,
        in_specs=(
            P(("sec", "col"), None, None),
            P(("sec", "col"), None, None),
            P(("sec", "col"), None, None, None),
            P(("sec", "col"), None),
            P("sec", None),
        ),
        out_specs=(P(("sec", "col"), None, None), P(("sec", "col"), None, None)),
        check_vma=False,
    )
```

```python
import functools

import jax
import jax.numpy as jnp
from jax import lax
from jax.experimental import pallas as pl
from jax.experimental.pallas import tpu as pltpu
from jax.sharding import PartitionSpec as P

MESH = pl.DeviceIdType.MESH


def low_size(n_col):
    low = 1
    while (2 * low) ** 2 <= n_col:
        low *= 2
    return low


def kernel(
    dims, targets_ref, slot_ref, rhs_hbm, diag_hbm, off_hbm, sol_ref, hand_ref,
    rhs_ref, diag_ref, off_ref, pack_ref, idx_vec, idx_ref, in_sem,
    a_ref, x_ref, inc, send1, recv1, send2, recv2, acc, passed,
    s1_sem, r1_sem, s2_sem, r2_sem, sp_sem, rp_sem,
):
    n_sec, n_hi, n_lo, chunks, nc = dims
    blocks, width, _ = rhs_ref.shape
    noff = off_ref.shape[1]
    rows = slot_ref.shape[1]
    lanes = idx_vec.shape[1]
    sec = lax.axis_index("sec")
    col = lax.axis_index("col")
    hi, lo = col // n_lo, col % n_lo
    size = blocks * width

    def lo_peer(o):
        return {"sec": sec, "col": hi * n_lo + lax.rem(lo + o, n_lo)}

    def hi_peer(o):
        return {"sec": sec, "col": lax.rem(hi + o, n_hi) * n_lo + lo}

    def next_sec():
        return {"sec": lax.rem(sec + 1, n_sec), "col": col}

    load_off = pltpu.make_async_copy(off_hbm, off_ref, in_sem.at[0])
    load_rhs = pltpu.make_async_copy(rhs_hbm, rhs_ref, in_sem.at[1])
    load_diag = pltpu.make_async_copy(diag_hbm, diag_ref, in_sem.at[2])
    load_off.start()
    load_rhs.start()
    load_diag.start()

    barrier = pltpu.get_barrier_semaphore()
    for o in range(1, n_lo):
        pl.semaphore_signal(barrier, inc=1, device_id=lo_peer(o), device_id_type=MESH)
    for o in range(1, n_hi):
        pl.semaphore_signal(barrier, inc=1, device_id=hi_peer(o), device_id_type=MESH)

    for by in (1, n_sec - 1):
        pl.semaphore_signal(
            barrier, inc=1, device_id={"sec": lax.rem(sec + by, n_sec), "col": col},
            device_id_type=MESH,
        )

    @pl.when(sec == 0)
    def _():
        inc[...] = jnp.zeros_like(inc)

    slot_of_lane = lax.broadcasted_iota(jnp.int32, (1, lanes), 1)
    for k in range(blocks):
        found = jnp.full((1, lanes), noff, jnp.int32)
        for p in range(noff):
            dest = slot_ref[0, targets_ref[k, p]]
            found = jnp.where(slot_of_lane == dest, p, found)
        idx_vec[k:k + 1, :] = found
    to_scalar = pltpu.make_async_copy(idx_vec, idx_ref, in_sem.at[3])
    to_scalar.start()

    pairs = blocks // 2
    load_off.wait()
    for q in range(pairs):
        pack_ref[q, noff] = jnp.zeros((width, 2 * width), jnp.bfloat16)

    def pack(p, carry):
        for q in range(pairs):
            pack_ref[q, p] = jnp.concatenate([off_ref[2 * q, p], off_ref[2 * q + 1, p]], axis=1)
        return carry

    lax.fori_loop(0, noff, pack, 0)
    to_scalar.wait()
    left = lax.broadcasted_iota(jnp.int32, (width, 2 * width), 1) < width

    def build(dest):
        for r in range(blocks):
            i = dest * blocks + r
            for q in range(pairs):
                a_ref[i, :, 2 * q * width:2 * (q + 1) * width] = jnp.where(
                    left, pack_ref[q, idx_ref[2 * q, i]], pack_ref[q, idx_ref[2 * q + 1, i]]
                )

    load_rhs.wait()
    load_diag.wait()
    pl.semaphore_wait(barrier, n_lo - 1 + n_hi - 1 + 2)

    def copy1(j, o, oh):
        return pltpu.make_async_remote_copy(
            src_ref=send1.at[j, o - 1, oh], dst_ref=recv1.at[j, o - 1, oh],
            send_sem=s1_sem.at[j, o - 1, oh], recv_sem=r1_sem.at[j, o - 1, oh],
            device_id=lo_peer(o), device_id_type=MESH,
        )

    def copy2(j, oh):
        return pltpu.make_async_remote_copy(
            src_ref=send2.at[j, oh - 1], dst_ref=recv2.at[j, oh - 1],
            send_sem=s2_sem.at[j, oh - 1], recv_sem=r2_sem.at[j, oh - 1],
            device_id=hi_peer(oh), device_id_type=MESH,
        )

    def copyp(j):
        return pltpu.make_async_remote_copy(
            src_ref=passed.at[j], dst_ref=inc.at[j],
            send_sem=sp_sem.at[j], recv_sem=rp_sem.at[j],
            device_id=next_sec(), device_id_type=MESH,
        )

    order = list(range(1, n_hi)) + [0]

    def product(j, oh, o):
        dest = lax.rem(hi + oh, n_hi) * n_lo + lax.rem(lo + o, n_lo)
        if j == 0:
            build(dest)
        a = a_ref[pl.ds(dest * blocks, blocks)].reshape(size, size)
        return jnp.dot(a, x_ref[j], preferred_element_type=jnp.float32)

    def first(j):
        @pl.when(sec > 0)
        def _():
            copyp(j).wait_recv()

        cols = slice(j * nc, (j + 1) * nc)
        for k in range(blocks):
            part = slice(k * width, (k + 1) * width)
            residual = (
                rhs_ref[k, :, cols].astype(jnp.float32) - inc[j, part, :].astype(jnp.float32)
            ).astype(jnp.bfloat16)
            solved = jnp.dot(
                diag_ref[k], residual, preferred_element_type=jnp.float32
            ).astype(jnp.bfloat16)
            x_ref[j, part, :] = solved
            sol_ref[k, :, cols] = solved
        for oh in order:
            for o in range(1, n_lo):
                send1[j, o - 1, oh] = product(j, oh, o).astype(jnp.bfloat16)
                copy1(j, o, oh).start()

    def middle(j):
        for oh in order:
            total = product(j, oh, 0)
            for o in range(1, n_lo):
                copy1(j, o, oh).wait_recv()
                total = total + recv1[j, o - 1, oh].astype(jnp.float32)
            if oh == 0:
                acc[j] = total
            else:
                send2[j, oh - 1] = total.astype(jnp.bfloat16)
                copy2(j, oh).start()

    def last(j):
        total = acc[j]
        for oh in range(1, n_hi):
            copy2(j, oh).wait_recv()
            total = total + recv2[j, oh - 1].astype(jnp.float32)
        passed[j] = total.astype(jnp.bfloat16)

        @pl.when(sec < n_sec - 1)
        def _():
            copyp(j).start()

        hand_ref[:, :, j * nc:(j + 1) * nc] = passed[j].reshape(blocks, width, nc)

    first(0)
    middle(0)
    for j in range(chunks):
        if j + 1 < chunks:
            first(j + 1)
        last(j)
        if j + 1 < chunks:
            middle(j + 1)

    for j in range(chunks):
        for o in range(1, n_lo):
            for oh in range(n_hi):
                copy1(j, o, oh).wait_send()
        for oh in range(1, n_hi):
            copy2(j, oh).wait_send()

        @pl.when(sec < n_sec - 1)
        def _():
            copyp(j).wait_send()


def shards(n_sec, n_col, rhs, diag_inv, off_tiles, targets, row_slot):
    blocks, width, columns = rhs.shape
    noff = off_tiles.shape[1]
    rows = row_slot.shape[1]
    n_lo = low_size(n_col)
    n_hi = n_col // n_lo
    nc = 128
    chunks = columns // nc
    size = blocks * width
    lanes = -(-rows // 128) * 128

    vmem = pl.BlockSpec(memory_space=pltpu.VMEM)
    smem = pl.BlockSpec(memory_space=pltpu.SMEM)
    hbm = pl.BlockSpec(memory_space=pl.ANY)
    out = jax.ShapeDtypeStruct((blocks, width, columns), jnp.bfloat16)
    dma = pltpu.SemaphoreType.DMA
    bf16 = jnp.bfloat16
    return pl.pallas_call(
        functools.partial(kernel, (n_sec, n_hi, n_lo, chunks, nc)),
        out_shape=(out, out),
        in_specs=[smem, smem, hbm, hbm, hbm],
        out_specs=(vmem, vmem),
        scratch_shapes=[
            pltpu.VMEM((blocks, width, columns), bf16),
            pltpu.VMEM((blocks, width, width), bf16),
            pltpu.VMEM((blocks, noff, width, width), bf16),
            pltpu.VMEM((blocks // 2, noff + 1, width, 2 * width), bf16),
            pltpu.VMEM((blocks, lanes), jnp.int32),
            pltpu.SMEM((blocks, lanes), jnp.int32),
            dma((4,)),
            pltpu.VMEM((rows, width, size), bf16),
            pltpu.VMEM((chunks, size, nc), bf16),
            pltpu.VMEM((chunks, size, nc), bf16),
            pltpu.VMEM((chunks, n_lo - 1, n_hi, size, nc), bf16),
            pltpu.VMEM((chunks, n_lo - 1, n_hi, size, nc), bf16),
            pltpu.VMEM((chunks, n_hi - 1, size, nc), bf16),
            pltpu.VMEM((chunks, n_hi - 1, size, nc), bf16),
            pltpu.VMEM((chunks, size, nc), jnp.float32),
            pltpu.VMEM((chunks, size, nc), bf16),
            dma((chunks, n_lo - 1, n_hi)),
            dma((chunks, n_lo - 1, n_hi)),
            dma((chunks, n_hi - 1)),
            dma((chunks, n_hi - 1)),
            dma((chunks,)),
            dma((chunks,)),
        ],
        compiler_params=pltpu.CompilerParams(
            collective_id=0, has_side_effects=True, vmem_limit_bytes=60 * 1024 * 1024
        ),
    )(targets, row_slot, rhs, diag_inv, off_tiles)


def solution(mesh):
    return jax.shard_map(
        functools.partial(shards, mesh.shape["sec"], mesh.shape["col"]),
        mesh=mesh,
        in_specs=(
            P(("sec", "col"), None, None),
            P(("sec", "col"), None, None),
            P(("sec", "col"), None, None, None),
            P(("sec", "col"), None),
            P("sec", None),
        ),
        out_specs=(P(("sec", "col"), None, None), P(("sec", "col"), None, None)),
        check_vma=False,
    )
```

```python
import functools

import jax
import jax.numpy as jnp
from jax import lax
from jax.experimental import pallas as pl
from jax.experimental.pallas import tpu as pltpu
from jax.sharding import PartitionSpec as P

MESH = pl.DeviceIdType.MESH
OWN, MIRROR, OTHER = 0, 1, 2


def low_size(n_col):
    low = 1
    while (2 * low) ** 2 <= n_col:
        low *= 2
    return low


def kernel(
    dims, targets_ref, slot_ref, rhs_hbm, diag_hbm, off_hbm, sol_ref, hand_ref,
    rin, diag_ref, off_ref, pack_own, pack_mirror, idx_vec, idx_ref,
    a_ref, x_ref, inc, send1, recv1, send2, recv2, acc, passed, ret,
    in_sem, fs_sem, fr_sem, s1_sem, r1_sem, s2_sem, r2_sem, sp_sem, rp_sem, sr_sem, rr_sem,
):
    n_sec, n_hi, n_lo = dims
    half = n_sec // 2
    blocks, width = off_hbm.shape[0], off_hbm.shape[2]
    noff = off_hbm.shape[1]
    rows = slot_ref.shape[1]
    lanes = idx_vec.shape[2]
    nc = rin.shape[3]
    size = blocks * width
    pairs = blocks // 2
    sec = lax.axis_index("sec")
    col = lax.axis_index("col")
    plane, place = sec // half, sec % half
    hi, lo = col // n_lo, col % n_lo
    mirror = {"sec": lax.rem(sec + half, n_sec), "col": col}

    def columns_of(which):
        return pl.ds(pl.multiple_of(which * nc, nc), nc)

    loads = [
        pltpu.make_async_copy(off_hbm, off_ref, in_sem.at[0]),
        pltpu.make_async_copy(diag_hbm, diag_ref.at[OWN], in_sem.at[1]),
        pltpu.make_async_copy(rhs_hbm.at[:, :, columns_of(plane)], rin.at[OWN], in_sem.at[2]),
        pltpu.make_async_copy(rhs_hbm.at[:, :, columns_of(1 - plane)], rin.at[OTHER], in_sem.at[3]),
    ]
    for load in loads:
        load.start()

    def lo_peer(o):
        return {"sec": sec, "col": hi * n_lo + lax.rem(lo + o, n_lo)}

    def hi_peer(o):
        return {"sec": sec, "col": lax.rem(hi + o, n_hi) * n_lo + lo}

    barrier = pltpu.get_barrier_semaphore()
    for o in range(1, n_lo):
        pl.semaphore_signal(barrier, inc=1, device_id=lo_peer(o), device_id_type=MESH)
    for o in range(1, n_hi):
        pl.semaphore_signal(barrier, inc=1, device_id=hi_peer(o), device_id_type=MESH)
    for o in range(1, n_sec):
        pl.semaphore_signal(
            barrier, inc=1, device_id={"sec": lax.rem(sec + o, n_sec), "col": col},
            device_id_type=MESH,
        )

    slot_of_lane = lax.broadcasted_iota(jnp.int32, (1, lanes), 1)
    for k in range(blocks):
        found = jnp.full((1, lanes), noff, jnp.int32)
        for p in range(noff):
            dest = slot_ref[0, targets_ref[k, p]]
            found = jnp.where(slot_of_lane == dest, p, found)
        idx_vec[OWN, k:k + 1, :] = found
    to_scalar = pltpu.make_async_copy(idx_vec.at[OWN], idx_ref.at[OWN], in_sem.at[4])
    to_scalar.start()

    packs = (pack_own, pack_mirror)
    for pack_ref in packs:
        for q in range(pairs):
            pack_ref[q, noff] = jnp.zeros((width, 2 * width), jnp.bfloat16)
    for load in loads:
        load.wait()

    def pack(p, carry):
        for q in range(pairs):
            pack_own[q, p] = jnp.concatenate([off_ref[2 * q, p], off_ref[2 * q + 1, p]], axis=1)
        return carry

    lax.fori_loop(0, noff, pack, 0)
    to_scalar.wait()
    pl.semaphore_wait(barrier, n_lo - 1 + n_hi - 1 + n_sec - 1)

    def factor_copies():
        ends = [
            (idx_vec.at[OWN], idx_vec.at[MIRROR]),
            (diag_ref.at[OWN], diag_ref.at[MIRROR]),
            (rin.at[OTHER], rin.at[MIRROR]),
        ] + [
            (pack_own.at[q, pl.ds(0, noff)], pack_mirror.at[q, pl.ds(0, noff)])
            for q in range(pairs)
        ]
        return [
            pltpu.make_async_remote_copy(
                src_ref=src, dst_ref=dst, send_sem=fs_sem.at[n], recv_sem=fr_sem.at[n],
                device_id=mirror, device_id_type=MESH,
            )
            for n, (src, dst) in enumerate(ends)
        ]

    @pl.when(sec != 0)
    def _():
        for copy in factor_copies():
            copy.start()

    def mirror_factor():
        for copy in factor_copies():
            copy.wait_recv()
        to_scalar = pltpu.make_async_copy(idx_vec.at[MIRROR], idx_ref.at[MIRROR], in_sem.at[5])
        to_scalar.start()
        to_scalar.wait()

    def source(role):
        return lax.rem(role + plane, 2)

    left = lax.broadcasted_iota(jnp.int32, (width, 2 * width), 1) < width

    def build_row(role, src, i):
        pack_ref = packs[src]
        for q in range(pairs):
            a_ref[role, i, :, 2 * q * width:2 * (q + 1) * width] = jnp.where(
                left,
                pack_ref[q, idx_ref[src, 2 * q, i]],
                pack_ref[q, idx_ref[src, 2 * q + 1, i]],
            )

    def build_all(role):
        for src in (OWN, MIRROR):
            @pl.when(source(role) == src)
            def _():
                def step(i, carry):
                    build_row(role, src, i)
                    return carry

                lax.fori_loop(0, rows, step, 0)

    def copy1(j, o, oh):
        return pltpu.make_async_remote_copy(
            src_ref=send1.at[j, o - 1, oh], dst_ref=recv1.at[j, o - 1, oh],
            send_sem=s1_sem.at[j, o - 1, oh], recv_sem=r1_sem.at[j, o - 1, oh],
            device_id=lo_peer(o), device_id_type=MESH,
        )

    def copy2(j, oh):
        return pltpu.make_async_remote_copy(
            src_ref=send2.at[j, oh - 1], dst_ref=recv2.at[j, oh - 1],
            send_sem=s2_sem.at[j, oh - 1], recv_sem=r2_sem.at[j, oh - 1],
            device_id=hi_peer(oh), device_id_type=MESH,
        )

    def copyp(j, to_sec, slot):
        return pltpu.make_async_remote_copy(
            src_ref=passed.at[j], dst_ref=inc.at[slot],
            send_sem=sp_sem.at[j], recv_sem=rp_sem.at[slot],
            device_id={"sec": to_sec, "col": col}, device_id_type=MESH,
        )

    def pass_on(j):
        if j == 0:
            return copyp(0, half + 1, 0)
        more = place + 1 < half
        to_sec = plane * half + jnp.where(more, place + 1, 0)
        if j == 1:
            return copyp(1, to_sec, jnp.where(more, 0, 1))
        return copyp(2, to_sec, 1)

    def give_back(which, j):
        return pltpu.make_async_remote_copy(
            src_ref=(x_ref, passed)[which].at[j], dst_ref=ret.at[which],
            send_sem=sr_sem.at[which], recv_sem=rr_sem.at[which],
            device_id=mirror, device_id_type=MESH,
        )

    order = list(range(1, n_hi)) + [0]

    def product(j, oh, o):
        role = max(j - 1, 0)
        dest = lax.rem(hi + oh, n_hi) * n_lo + lax.rem(lo + o, n_lo)
        if j == 0:
            for r in range(blocks):
                build_row(0, OWN, dest * blocks + r)
        a = a_ref[role, pl.ds(dest * blocks, blocks)].reshape(size, size)
        return jnp.dot(a, x_ref[j], preferred_element_type=jnp.float32)

    def first(j, fresh):
        role = max(j - 1, 0)
        src = source(role)
        which = OTHER if j == 0 else src
        if not fresh:
            copyp(j, sec, role).wait_recv()
        for k in range(blocks):
            part = slice(k * width, (k + 1) * width)
            residual = rin[which, k]
            if not fresh:
                residual = (
                    residual.astype(jnp.float32) - inc[role, part, :].astype(jnp.float32)
                ).astype(jnp.bfloat16)
            x_ref[j, part, :] = jnp.dot(
                diag_ref[src, k], residual, preferred_element_type=jnp.float32
            ).astype(jnp.bfloat16)
        for oh in order:
            for o in range(1, n_lo):
                send1[j, o - 1, oh] = product(j, oh, o).astype(jnp.bfloat16)
                copy1(j, o, oh).start()

    def middle(j):
        for oh in order:
            total = product(j, oh, 0)
            for o in range(1, n_lo):
                copy1(j, o, oh).wait_recv()
                total = total + recv1[j, o - 1, oh].astype(jnp.float32)
            if oh == 0:
                acc[j] = total
            else:
                send2[j, oh - 1] = total.astype(jnp.bfloat16)
                copy2(j, oh).start()

    def last(j):
        total = acc[j]
        for oh in range(1, n_hi):
            copy2(j, oh).wait_recv()
            total = total + recv2[j, oh - 1].astype(jnp.float32)
        passed[j] = total.astype(jnp.bfloat16)
        if j < 2:
            pass_on(j).start()
        else:
            @pl.when(place < half - 1)
            def _():
                pass_on(j).start()

        if j > 0:
            @pl.when(source(j - 1) == MIRROR)
            def _():
                give_back(0, j).start()
                give_back(1, j).start()

    def sent(j):
        for oh in range(n_hi):
            for o in range(1, n_lo):
                copy1(j, o, oh).wait_send()
        for oh in range(1, n_hi):
            copy2(j, oh).wait_send()

    @pl.when(sec == 0)
    def _():
        first(0, True)
        middle(0)
        first(1, True)
        last(0)
        middle(1)
        last(1)
        sent(0)
        sent(1)
        pass_on(0).wait_send()
        pass_on(1).wait_send()

    @pl.when(place > 0)
    def _():
        @pl.when(plane == 1)
        def _():
            mirror_factor()

        build_all(0)
        first(1, False)
        middle(1)
        last(1)
        sent(1)
        pass_on(1).wait_send()

    @pl.when(plane == 0)
    def _():
        mirror_factor()

    build_all(1)
    first(2, False)
    middle(2)
    last(2)
    own = 1 + plane
    sol_ref[:, :, columns_of(plane)] = x_ref[own].reshape(blocks, width, nc)
    hand_ref[:, :, columns_of(plane)] = passed[own].reshape(blocks, width, nc)

    @pl.when(sec == 0)
    def _():
        sol_ref[:, :, nc:2 * nc] = x_ref[0].reshape(blocks, width, nc)
        hand_ref[:, :, nc:2 * nc] = passed[0].reshape(blocks, width, nc)

    @pl.when(sec != 0)
    def _():
        give_back(0, 1).wait_recv()
        sol_ref[:, :, columns_of(1 - plane)] = ret[0].reshape(blocks, width, nc)
        give_back(1, 1).wait_recv()
        hand_ref[:, :, columns_of(1 - plane)] = ret[1].reshape(blocks, width, nc)
        for copy in factor_copies():
            copy.wait_send()

    sent(2)

    @pl.when(place < half - 1)
    def _():
        pass_on(2).wait_send()

    @pl.when(sec != half)
    def _():
        give_back(0, 1).wait_send()
        give_back(1, 1).wait_send()


def shards(n_sec, n_col, rhs, diag_inv, off_tiles, targets, row_slot):
    blocks, width, columns = rhs.shape
    noff = off_tiles.shape[1]
    rows = row_slot.shape[1]
    n_lo = low_size(n_col)
    n_hi = n_col // n_lo
    nc = columns // 2
    size = blocks * width
    pairs = blocks // 2
    lanes = -(-rows // 128) * 128

    vmem = pl.BlockSpec(memory_space=pltpu.VMEM)
    smem = pl.BlockSpec(memory_space=pltpu.SMEM)
    hbm = pl.BlockSpec(memory_space=pl.ANY)
    out = jax.ShapeDtypeStruct((blocks, width, columns), jnp.bfloat16)
    dma = pltpu.SemaphoreType.DMA
    bf16 = jnp.bfloat16
    return pl.pallas_call(
        functools.partial(kernel, (n_sec, n_hi, n_lo)),
        out_shape=(out, out),
        in_specs=[smem, smem, hbm, hbm, hbm],
        out_specs=(vmem, vmem),
        scratch_shapes=[
            pltpu.VMEM((3, blocks, width, nc), bf16),
            pltpu.VMEM((2, blocks, width, width), bf16),
            pltpu.VMEM((blocks, noff, width, width), bf16),
            pltpu.VMEM((pairs, noff + 1, width, 2 * width), bf16),
            pltpu.VMEM((pairs, noff + 1, width, 2 * width), bf16),
            pltpu.VMEM((2, blocks, lanes), jnp.int32),
            pltpu.SMEM((2, blocks, lanes), jnp.int32),
            pltpu.VMEM((2, rows, width, size), bf16),
            pltpu.VMEM((3, size, nc), bf16),
            pltpu.VMEM((2, size, nc), bf16),
            pltpu.VMEM((3, n_lo - 1, n_hi, size, nc), bf16),
            pltpu.VMEM((3, n_lo - 1, n_hi, size, nc), bf16),
            pltpu.VMEM((3, n_hi - 1, size, nc), bf16),
            pltpu.VMEM((3, n_hi - 1, size, nc), bf16),
            pltpu.VMEM((3, size, nc), jnp.float32),
            pltpu.VMEM((3, size, nc), bf16),
            pltpu.VMEM((2, size, nc), bf16),
            dma((6,)),
            dma((3 + pairs,)),
            dma((3 + pairs,)),
            dma((3, n_lo - 1, n_hi)),
            dma((3, n_lo - 1, n_hi)),
            dma((3, n_hi - 1)),
            dma((3, n_hi - 1)),
            dma((3,)),
            dma((2,)),
            dma((2,)),
            dma((2,)),
        ],
        compiler_params=pltpu.CompilerParams(
            collective_id=0, has_side_effects=True, vmem_limit_bytes=60 * 1024 * 1024
        ),
    )(targets, row_slot, rhs, diag_inv, off_tiles)


def solution(mesh):
    return jax.shard_map(
        functools.partial(shards, mesh.shape["sec"], mesh.shape["col"]),
        mesh=mesh,
        in_specs=(
            P(("sec", "col"), None, None),
            P(("sec", "col"), None, None),
            P(("sec", "col"), None, None, None),
            P(("sec", "col"), None),
            P("sec", None),
        ),
        out_specs=(P(("sec", "col"), None, None), P(("sec", "col"), None, None)),
        check_vma=False,
    )
```

```python
import functools

import jax
import jax.numpy as jnp
from jax import lax
from jax.experimental import pallas as pl
from jax.experimental.pallas import tpu as pltpu
from jax.sharding import PartitionSpec as P

MESH = pl.DeviceIdType.MESH
OWN, MIRROR, OTHER = 0, 1, 2


def low_size(n_col):
    low = 1
    while (2 * low) ** 2 <= n_col:
        low *= 2
    return low


def kernel(
    dims, targets_ref, slot_ref, rhs_hbm, diag_hbm, off_hbm, sol_ref, hand_ref,
    rin, diag_ref, off_ref, pack_own, pack_mirror, idx_vec, idx_ref,
    a_ref, x_ref, inc, send1, recv1, send2, recv2, acc, passed, ret,
    in_sem, fs_sem, fr_sem, s1_sem, r1_sem, s2_sem, r2_sem, sp_sem, rp_sem, sr_sem, rr_sem,
):
    n_sec, n_hi, n_lo = dims
    half = n_sec // 2
    blocks, width = off_hbm.shape[0], off_hbm.shape[2]
    noff = off_hbm.shape[1]
    rows = slot_ref.shape[1]
    lanes = idx_vec.shape[2]
    nc = rin.shape[3]
    size = blocks * width
    pairs = blocks // 2
    sec = lax.axis_index("sec")
    col = lax.axis_index("col")
    plane, place = sec // half, sec % half
    hi, lo = col // n_lo, col % n_lo
    mirror = {"sec": lax.rem(sec + half, n_sec), "col": col}

    def columns_of(which):
        return pl.ds(pl.multiple_of(which * nc, nc), nc)

    loads = [
        pltpu.make_async_copy(off_hbm, off_ref, in_sem.at[0]),
        pltpu.make_async_copy(diag_hbm, diag_ref.at[OWN], in_sem.at[1]),
        pltpu.make_async_copy(rhs_hbm.at[:, :, columns_of(plane)], rin.at[OWN], in_sem.at[2]),
        pltpu.make_async_copy(rhs_hbm.at[:, :, columns_of(1 - plane)], rin.at[OTHER], in_sem.at[3]),
    ]
    for load in loads:
        load.start()

    def lo_peer(o):
        return {"sec": sec, "col": hi * n_lo + lax.rem(lo + o, n_lo)}

    def hi_flip(o):
        value, bit = hi, 1
        while bit < n_hi:
            if o & bit:
                value = value + bit - 2 * bit * ((value // bit) % 2)
            bit *= 2
        return value

    def hi_peer(o):
        return {"sec": sec, "col": hi_flip(o) * n_lo + lo}

    barrier = pltpu.get_barrier_semaphore()
    for o in range(1, n_lo):
        pl.semaphore_signal(barrier, inc=1, device_id=lo_peer(o), device_id_type=MESH)
    for o in range(1, n_hi):
        pl.semaphore_signal(barrier, inc=1, device_id=hi_peer(o), device_id_type=MESH)
    for o in range(1, n_sec):
        pl.semaphore_signal(
            barrier, inc=1, device_id={"sec": lax.rem(sec + o, n_sec), "col": col},
            device_id_type=MESH,
        )

    slot_of_lane = lax.broadcasted_iota(jnp.int32, (1, lanes), 1)
    for k in range(blocks):
        found = jnp.full((1, lanes), noff, jnp.int32)
        for p in range(noff):
            dest = slot_ref[0, targets_ref[k, p]]
            found = jnp.where(slot_of_lane == dest, p, found)
        idx_vec[OWN, k:k + 1, :] = found
    to_scalar = pltpu.make_async_copy(idx_vec.at[OWN], idx_ref.at[OWN], in_sem.at[4])
    to_scalar.start()

    packs = (pack_own, pack_mirror)
    for pack_ref in packs:
        for q in range(pairs):
            pack_ref[q, noff] = jnp.zeros((width, 2 * width), jnp.bfloat16)
    for load in loads:
        load.wait()

    def pack(p, carry):
        for q in range(pairs):
            pack_own[q, p] = jnp.concatenate([off_ref[2 * q, p], off_ref[2 * q + 1, p]], axis=1)
        return carry

    lax.fori_loop(0, noff, pack, 0)
    to_scalar.wait()
    pl.semaphore_wait(barrier, n_lo - 1 + n_hi - 1 + n_sec - 1)

    def factor_copies():
        ends = [
            (idx_vec.at[OWN], idx_vec.at[MIRROR]),
            (diag_ref.at[OWN], diag_ref.at[MIRROR]),
            (rin.at[OTHER], rin.at[MIRROR]),
        ] + [
            (pack_own.at[q, pl.ds(0, noff)], pack_mirror.at[q, pl.ds(0, noff)])
            for q in range(pairs)
        ]
        return [
            pltpu.make_async_remote_copy(
                src_ref=src, dst_ref=dst, send_sem=fs_sem.at[n], recv_sem=fr_sem.at[n],
                device_id=mirror, device_id_type=MESH,
            )
            for n, (src, dst) in enumerate(ends)
        ]

    @pl.when(sec != 0)
    def _():
        for copy in factor_copies():
            copy.start()

    def mirror_factor():
        for copy in factor_copies():
            copy.wait_recv()
        to_scalar = pltpu.make_async_copy(idx_vec.at[MIRROR], idx_ref.at[MIRROR], in_sem.at[5])
        to_scalar.start()
        to_scalar.wait()

    def source(role):
        return lax.rem(role + plane, 2)

    left = lax.broadcasted_iota(jnp.int32, (width, 2 * width), 1) < width

    def build_row(role, src, i):
        pack_ref = packs[src]
        for q in range(pairs):
            a_ref[role, i, :, 2 * q * width:2 * (q + 1) * width] = jnp.where(
                left,
                pack_ref[q, idx_ref[src, 2 * q, i]],
                pack_ref[q, idx_ref[src, 2 * q + 1, i]],
            )

    def build_all(role):
        for src in (OWN, MIRROR):
            @pl.when(source(role) == src)
            def _():
                def step(i, carry):
                    build_row(role, src, i)
                    return carry

                lax.fori_loop(0, rows, step, 0)

    def copy1(j, o, oh):
        return pltpu.make_async_remote_copy(
            src_ref=send1.at[j, o - 1, oh], dst_ref=recv1.at[j, o - 1, oh],
            send_sem=s1_sem.at[j, o - 1, oh], recv_sem=r1_sem.at[j, o - 1, oh],
            device_id=lo_peer(o), device_id_type=MESH,
        )

    def copy2(j, oh):
        return pltpu.make_async_remote_copy(
            src_ref=send2.at[j, oh - 1], dst_ref=recv2.at[j, oh - 1],
            send_sem=s2_sem.at[j, oh - 1], recv_sem=r2_sem.at[j, oh - 1],
            device_id=hi_peer(oh), device_id_type=MESH,
        )

    def copyp(j, to_sec, slot):
        return pltpu.make_async_remote_copy(
            src_ref=passed.at[j], dst_ref=inc.at[slot],
            send_sem=sp_sem.at[j], recv_sem=rp_sem.at[slot],
            device_id={"sec": to_sec, "col": col}, device_id_type=MESH,
        )

    def pass_on(j):
        if j == 0:
            return copyp(0, half + 1, 0)
        more = place + 1 < half
        to_sec = plane * half + jnp.where(more, place + 1, 0)
        if j == 1:
            return copyp(1, to_sec, jnp.where(more, 0, 1))
        return copyp(2, to_sec, 1)

    def give_back(which, j):
        return pltpu.make_async_remote_copy(
            src_ref=(x_ref, passed)[which].at[j], dst_ref=ret.at[which],
            send_sem=sr_sem.at[which], recv_sem=rr_sem.at[which],
            device_id=mirror, device_id_type=MESH,
        )

    order = list(range(n_hi - 1, -1, -1))

    def product(j, oh, o):
        role = max(j - 1, 0)
        dest = hi_flip(oh) * n_lo + lax.rem(lo + o, n_lo)
        if j == 0:
            for r in range(blocks):
                build_row(0, OWN, dest * blocks + r)
        a = a_ref[role, pl.ds(dest * blocks, blocks)].reshape(size, size)
        return jnp.dot(a, x_ref[j], preferred_element_type=jnp.float32)

    def first(j, fresh):
        role = max(j - 1, 0)
        src = source(role)
        which = OTHER if j == 0 else src
        if not fresh:
            copyp(j, sec, role).wait_recv()
        for k in range(blocks):
            part = slice(k * width, (k + 1) * width)
            residual = rin[which, k]
            if not fresh:
                residual = (
                    residual.astype(jnp.float32) - inc[role, part, :].astype(jnp.float32)
                ).astype(jnp.bfloat16)
            x_ref[j, part, :] = jnp.dot(
                diag_ref[src, k], residual, preferred_element_type=jnp.float32
            ).astype(jnp.bfloat16)
        for oh in order:
            for o in range(1, n_lo):
                send1[j, o - 1, oh] = product(j, oh, o).astype(jnp.bfloat16)
                copy1(j, o, oh).start()

    def middle(j):
        for oh in order:
            total = product(j, oh, 0)
            for o in range(1, n_lo):
                copy1(j, o, oh).wait_recv()
                total = total + recv1[j, o - 1, oh].astype(jnp.float32)
            if oh == 0:
                acc[j] = total
            else:
                send2[j, oh - 1] = total.astype(jnp.bfloat16)
                copy2(j, oh).start()

    def last(j):
        total = acc[j]
        for oh in range(1, n_hi):
            copy2(j, oh).wait_recv()
            total = total + recv2[j, oh - 1].astype(jnp.float32)
        passed[j] = total.astype(jnp.bfloat16)
        if j < 2:
            pass_on(j).start()
        else:
            @pl.when(place < half - 1)
            def _():
                pass_on(j).start()

        if j > 0:
            @pl.when(source(j - 1) == MIRROR)
            def _():
                give_back(0, j).start()
                give_back(1, j).start()

    def sent(j):
        for oh in range(n_hi):
            for o in range(1, n_lo):
                copy1(j, o, oh).wait_send()
        for oh in range(1, n_hi):
            copy2(j, oh).wait_send()

    @pl.when(sec == 0)
    def _():
        first(0, True)
        middle(0)
        first(1, True)
        last(0)
        middle(1)
        last(1)
        sent(0)
        sent(1)
        pass_on(0).wait_send()
        pass_on(1).wait_send()

    @pl.when(place > 0)
    def _():
        @pl.when(plane == 1)
        def _():
            mirror_factor()

        build_all(0)
        first(1, False)
        middle(1)
        last(1)
        sent(1)
        pass_on(1).wait_send()

    @pl.when(plane == 0)
    def _():
        mirror_factor()

    build_all(1)
    first(2, False)
    middle(2)
    last(2)
    own = 1 + plane
    sol_ref[:, :, columns_of(plane)] = x_ref[own].reshape(blocks, width, nc)
    hand_ref[:, :, columns_of(plane)] = passed[own].reshape(blocks, width, nc)

    @pl.when(sec == 0)
    def _():
        sol_ref[:, :, nc:2 * nc] = x_ref[0].reshape(blocks, width, nc)
        hand_ref[:, :, nc:2 * nc] = passed[0].reshape(blocks, width, nc)

    @pl.when(sec != 0)
    def _():
        give_back(0, 1).wait_recv()
        sol_ref[:, :, columns_of(1 - plane)] = ret[0].reshape(blocks, width, nc)
        give_back(1, 1).wait_recv()
        hand_ref[:, :, columns_of(1 - plane)] = ret[1].reshape(blocks, width, nc)
        for copy in factor_copies():
            copy.wait_send()

    sent(2)

    @pl.when(place < half - 1)
    def _():
        pass_on(2).wait_send()

    @pl.when(sec != half)
    def _():
        give_back(0, 1).wait_send()
        give_back(1, 1).wait_send()


def shards(n_sec, n_col, rhs, diag_inv, off_tiles, targets, row_slot):
    blocks, width, columns = rhs.shape
    noff = off_tiles.shape[1]
    rows = row_slot.shape[1]
    n_lo = low_size(n_col)
    n_hi = n_col // n_lo
    nc = columns // 2
    size = blocks * width
    pairs = blocks // 2
    lanes = -(-rows // 128) * 128

    vmem = pl.BlockSpec(memory_space=pltpu.VMEM)
    smem = pl.BlockSpec(memory_space=pltpu.SMEM)
    hbm = pl.BlockSpec(memory_space=pl.ANY)
    out = jax.ShapeDtypeStruct((blocks, width, columns), jnp.bfloat16)
    dma = pltpu.SemaphoreType.DMA
    bf16 = jnp.bfloat16
    return pl.pallas_call(
        functools.partial(kernel, (n_sec, n_hi, n_lo)),
        out_shape=(out, out),
        in_specs=[smem, smem, hbm, hbm, hbm],
        out_specs=(vmem, vmem),
        scratch_shapes=[
            pltpu.VMEM((3, blocks, width, nc), bf16),
            pltpu.VMEM((2, blocks, width, width), bf16),
            pltpu.VMEM((blocks, noff, width, width), bf16),
            pltpu.VMEM((pairs, noff + 1, width, 2 * width), bf16),
            pltpu.VMEM((pairs, noff + 1, width, 2 * width), bf16),
            pltpu.VMEM((2, blocks, lanes), jnp.int32),
            pltpu.SMEM((2, blocks, lanes), jnp.int32),
            pltpu.VMEM((2, rows, width, size), bf16),
            pltpu.VMEM((3, size, nc), bf16),
            pltpu.VMEM((2, size, nc), bf16),
            pltpu.VMEM((3, n_lo - 1, n_hi, size, nc), bf16),
            pltpu.VMEM((3, n_lo - 1, n_hi, size, nc), bf16),
            pltpu.VMEM((3, n_hi - 1, size, nc), bf16),
            pltpu.VMEM((3, n_hi - 1, size, nc), bf16),
            pltpu.VMEM((3, size, nc), jnp.float32),
            pltpu.VMEM((3, size, nc), bf16),
            pltpu.VMEM((2, size, nc), bf16),
            dma((6,)),
            dma((3 + pairs,)),
            dma((3 + pairs,)),
            dma((3, n_lo - 1, n_hi)),
            dma((3, n_lo - 1, n_hi)),
            dma((3, n_hi - 1)),
            dma((3, n_hi - 1)),
            dma((3,)),
            dma((2,)),
            dma((2,)),
            dma((2,)),
        ],
        compiler_params=pltpu.CompilerParams(
            collective_id=0, has_side_effects=True, vmem_limit_bytes=60 * 1024 * 1024
        ),
    )(targets, row_slot, rhs, diag_inv, off_tiles)


def solution(mesh):
    return jax.shard_map(
        functools.partial(shards, mesh.shape["sec"], mesh.shape["col"]),
        mesh=mesh,
        in_specs=(
            P(("sec", "col"), None, None),
            P(("sec", "col"), None, None),
            P(("sec", "col"), None, None, None),
            P(("sec", "col"), None),
            P("sec", None),
        ),
        out_specs=(P(("sec", "col"), None, None), P(("sec", "col"), None, None)),
        check_vma=False,
    )
```
